256 devices in a mesh: dx: 32 (over z, x_lo, core), dy: 8 (over x_hi, y).
Axes of the slice: x: 4 (x_hi: 2, x_lo: 2; x = x_hi * 2 + x_lo), y: 4, z: 8, core: 2. Of those that a mesh axis runs over, the one named last changes fastest.
Arguments:
- img_emb: bfloat16 [131072, 1152], P(('dx', 'dy')), may hold values from -0.1796875 to 0.1796875
- txt_emb: bfloat16 [131072, 1152], P(('dx', 'dy')), may hold values from -0.1796875 to 0.1796875
- logit_scale: float32 [1], replicated, may hold values from 4 to 8
- logit_bias: float32 [1], replicated, may hold values from -3 to -1
Outputs:
- grad_img: float32 [131072, 1152], P(('dx', 'dy'))
- grad_txt: float32 [131072, 1152], P(('dx', 'dy'))
The draws below stay inside these ranges and needn't reach their ends.
All inputs are finite; a program needn't handle non-finite values.
Results may differ from the reference program's by a relative error of at most 0.0049.
Values may be sent and summed in bfloat16 or wider, within the bound.
A program may use at most 64 MiB of HBM per device.

```python
import jax
import jax.numpy as jnp
from jax import lax

E = 1152
ROWS = 512
PAIRS = 131072
N_DX = 32
N_DY = 8


def levels(own_key, dims, pieces, least, top_value):
    factor_of, own = 1.0, jax.random.fold_in(own_key, 6)
    for axis_at, blocks in pieces:
        draws = jnp.exp(jax.random.uniform(jax.random.fold_in(own, axis_at), (blocks,), jnp.float32, least / len(pieces), top_value / len(pieces)))
        factor_of = factor_of * jnp.repeat(draws, dims[axis_at] // blocks).reshape([-1 if axis == axis_at else 1 for axis in range(len(dims))])
    return factor_of


def normal_values(rng, dims, scale, limit, split=(), held_as=jnp.bfloat16):
    array = jax.random.normal(rng, dims, jnp.float32) * scale
    if len(split) > 0:
        array = levels(rng, dims, split, -0.22, 0.18) * array
    return jnp.clip(array, min=-limit, max=limit).astype(held_as)


def setup_inputs(seed: int = 0) -> dict:
    keys = jax.random.split(jax.random.key(seed), 5)
    return {
        "img_emb": normal_values(keys[0], (PAIRS, E), 0.03, 0.1796875, ((0, 256),)),
        "txt_emb": normal_values(keys[1], (PAIRS, E), 0.03, 0.1796875, ((0, 256),)),
        "logit_scale": jnp.clip(jax.random.uniform(keys[2], (1,), jnp.float32, 4.0, 8.0), 4.0, 8.0),
        "logit_bias": jnp.clip(jax.random.uniform(keys[3], (1,), jnp.float32, -3.0, -1.0), -3.0, -1.0),
    }


def normalize(values):
    floats = values.astype(jnp.float32)
    inverse = lax.rsqrt(lax.optimization_barrier(jnp.sum(floats * floats, axis=-1, keepdims=True)) + 1e-06)
    return (floats * inverse, inverse)

def tile_weights(images, texts, scale, bias, diagonal):
    logits = scale * jnp.dot(images, texts.T, preferred_element_type=jnp.float32) + bias
    if diagonal:
        eye = jnp.arange(images.shape[0])[:, None] == jnp.arange(texts.shape[0])[None, :]
        signs = jnp.where(eye, jnp.float32(1.0), jnp.float32(-1.0))
    else:
        signs = jnp.full(logits.shape, -1.0, jnp.float32)
    coeffs = -signs * jax.nn.sigmoid(-signs * logits)
    return (scale * coeffs).astype(jnp.bfloat16)

def finish(unit, inverse, grads):
    return inverse * (grads - unit * lax.optimization_barrier(jnp.sum(unit * grads, axis=-1, keepdims=True)))

def reference(img_emb, txt_emb, logit_scale, logit_bias):
    blocks_all = N_DX * N_DY
    img_unit, inv_img = normalize(img_emb)
    txt_unit, inv_txt = normalize(txt_emb)
    img_b = img_unit.astype(jnp.bfloat16).reshape(blocks_all, ROWS, E)
    txt_b = txt_unit.astype(jnp.bfloat16).reshape(blocks_all, ROWS, E)
    scale = logit_scale[0]
    bias = logit_bias[0]

    def own_tile(blocks):
        images, texts = blocks
        coeffs = tile_weights(images, texts, scale, bias, True)
        return (jnp.dot(coeffs, texts, preferred_element_type=jnp.float32), jnp.dot(coeffs.T, images, preferred_element_type=jnp.float32))
    grad_i, grad_t = lax.map(own_tile, (img_b, txt_b))

    def cross_tile(blocks):
        images, texts = blocks
        coeffs = tile_weights(images, texts, scale, bias, False)
        return (jnp.dot(coeffs, texts, preferred_element_type=jnp.float32), jnp.dot(coeffs.T, images, preferred_element_type=jnp.float32).astype(jnp.bfloat16))
    for mask_value in [1, N_DY, N_DX // 2 * N_DY, 2 * N_DY]:
        partner = jnp.bitwise_xor(jnp.arange(blocks_all, dtype=jnp.int32), jnp.int32(mask_value))
        grad_more, partial_value = lax.map(cross_tile, (img_b, txt_b[partner]))
        partial_value = lax.optimization_barrier(partial_value)
        grad_i = grad_i + grad_more
        grad_t = grad_t + partial_value[partner].astype(jnp.float32)
    grad_i = grad_i.reshape(blocks_all * ROWS, E)
    grad_t = grad_t.reshape(blocks_all * ROWS, E)
    return (finish(img_unit, inv_img, grad_i), finish(txt_unit, inv_txt, grad_t))
```

```python
import functools

import jax
import jax.numpy as jnp
from jax import lax
from jax.experimental import pallas as pl
from jax.experimental.pallas import tpu as pltpu
from jax.sharding import PartitionSpec as P

ROWS = 512
E = 1152
STEP = 256
Z_ROWS = 128
FINISH_ROWS = 128
IMG, TXT = 0, 1
CORE, Y, X, Z = 0, 1, 2, 3


def flipped(index, bit):
    return jnp.where(lax.rem(index // bit, 2) == 1, index - bit, index + bit)


def projected(grads, raw, inverse):
    units = raw.astype(jnp.float32) * inverse
    return inverse * (grads - units * jnp.sum(units * grads, axis=-1, keepdims=True))


def unit_rows(values):
    floats = values.astype(jnp.float32)
    inverse = lax.rsqrt(jnp.sum(floats * floats, axis=-1, keepdims=True) + 1e-06)
    return floats * inverse, inverse


def gather_kernel(n_dx, img, txt, scale_ref, bias_ref, out_img, out_txt, raw, inv, unit, far,
                  load_sem, send_sem, recv_sem, z_send, z_recv):
    dx, dy = lax.axis_index("dx"), lax.axis_index("dy")
    partners = (
        (flipped(dx, 1), dy),
        (dx, flipped(dy, 1)),
        (flipped(dx, 2), dy),
        (flipped(dx, n_dx // 2), dy),
    )
    scale, bias = scale_ref[0], bias_ref[0]
    blocks = (img, txt)
    outs = (out_img, out_txt)

    loads = [pltpu.make_async_copy(blocks[kind], raw.at[kind], load_sem.at[kind]) for kind in (IMG, TXT)]
    for load in loads:
        load.start()

    barrier = pltpu.get_barrier_semaphore()
    for partner in partners:
        pl.semaphore_signal(barrier, inc=1, device_id=partner, device_id_type=pl.DeviceIdType.MESH)
    pl.semaphore_wait(barrier, 4)

    z_copies, copies = {}, {}
    per_kind = ROWS // Z_ROWS
    for kind in (TXT, IMG):
        for part in range(per_kind):
            rows = pl.ds(part * Z_ROWS, Z_ROWS)
            z_copies[kind, part] = pltpu.make_async_remote_copy(
                src_ref=blocks[kind].at[rows],
                dst_ref=far.at[Z, kind, rows],
                send_sem=z_send.at[kind, part],
                recv_sem=z_recv.at[kind, part],
                device_id=partners[Z],
                device_id_type=pl.DeviceIdType.MESH,
            )
    for kind in (TXT, IMG):
        for part in range(per_kind):
            z_copies[kind, part].start()
    for kind in (TXT, IMG):
        for way in (Y, X, CORE):
            copies[way, kind] = pltpu.make_async_remote_copy(
                src_ref=blocks[kind],
                dst_ref=far.at[way, kind],
                send_sem=send_sem.at[way, kind],
                recv_sem=recv_sem.at[way, kind],
                device_id=partners[way],
                device_id_type=pl.DeviceIdType.MESH,
            )
            copies[way, kind].start()

    for load in loads:
        load.wait()

    @pl.loop(0, ROWS // 128)
    def _(step):
        rows = pl.ds(step * 128, 128)
        for kind in (IMG, TXT):
            units, inverse = unit_rows(raw[kind, rows, :])
            unit[kind, rows, :] = units.astype(jnp.bfloat16)
            inv[kind, rows, :] = inverse

    def tile(kind, others, row, diagonal=None):
        mine = 1 - kind
        rows = pl.ds(row, STEP)
        logits = scale * lax.dot_general(
            unit[mine, rows, :], others, (((1,), (1,)), ((), ())), preferred_element_type=jnp.float32
        ) + bias
        if diagonal is None:
            coeffs = jax.nn.sigmoid(logits)
        else:
            first = row + lax.broadcasted_iota(jnp.int32, logits.shape, 0)
            second = diagonal + lax.broadcasted_iota(jnp.int32, logits.shape, 1)
            signs = jnp.where(first == second, jnp.float32(1.0), jnp.float32(-1.0))
            coeffs = -signs * jax.nn.sigmoid(-signs * logits)
        return jnp.dot((scale * coeffs).astype(jnp.bfloat16), others, preferred_element_type=jnp.float32)

    for kind in (TXT, IMG):
        mine = 1 - kind
        for row in range(0, ROWS, STEP):
            outs[mine][row : row + STEP, :] = tile(kind, unit[kind, 0:STEP, :], row, 0)
            outs[mine][row : row + STEP, :] += tile(kind, unit[kind, STEP:ROWS, :], row, STEP)

    def add_tiles(way, kind, start, count):
        mine = 1 - kind
        others = unit_rows(far[way, kind, pl.ds(start, count), :])[0].astype(jnp.bfloat16)
        for row in range(0, ROWS, STEP):
            outs[mine][row : row + STEP, :] += tile(kind, others, row)

    for way in (CORE, Y, X):
        for kind in (TXT, IMG):
            copies[way, kind].wait_recv()

            @pl.loop(0, ROWS // STEP)
            def _(step):
                add_tiles(way, kind, step * STEP, STEP)

    for kind in (TXT, IMG):
        for part in range(per_kind):
            z_copies[kind, part].wait_recv()
            add_tiles(Z, kind, part * Z_ROWS, Z_ROWS)
        if kind == TXT:

            @pl.loop(0, ROWS // 128)
            def _(step):
                rows = pl.ds(step * 128, 128)
                out_img[rows, :] = projected(out_img[rows, :], raw[IMG, rows, :], inv[IMG, rows, :])

    for copy in (*z_copies.values(), *copies.values()):
        copy.wait_send()


def finish_kernel(grad_img, sum_txt, raw, inv, out_img, out_txt, grad_txt, sem):
    whole = pltpu.make_async_copy(grad_img, out_img, sem.at[0])
    whole.start()
    parts = []
    for part in range(ROWS // FINISH_ROWS):
        rows = pl.ds(part * FINISH_ROWS, FINISH_ROWS)
        grad_txt[rows, :] = projected(sum_txt[rows, :], raw[TXT, rows, :], inv[TXT, rows, :])
        parts.append(pltpu.make_async_copy(grad_txt.at[rows], out_txt.at[rows], sem.at[1 + part]))
        parts[-1].start()
    for copy in (whole, *parts):
        copy.wait()


def per_device(n_dx, img_emb, txt_emb, logit_scale, logit_bias):
    per_kind = ROWS // Z_ROWS
    vmem = pl.BlockSpec(memory_space=pltpu.VMEM)
    img_emb = pltpu.with_memory_space_constraint(img_emb, pltpu.HBM)
    txt_emb = pltpu.with_memory_space_constraint(txt_emb, pltpu.HBM)
    sums = pl.pallas_call(
        functools.partial(gather_kernel, n_dx),
        out_shape=(
            pltpu.VMEM((ROWS, E), jnp.float32),
            pltpu.VMEM((ROWS, E), jnp.float32),
            pltpu.VMEM((2, ROWS, E), jnp.bfloat16),
            pltpu.VMEM((2, ROWS, 1), jnp.float32),
        ),
        in_specs=[pl.BlockSpec(memory_space=pltpu.HBM)] * 2 + [pl.BlockSpec(memory_space=pltpu.SMEM)] * 2,
        out_specs=[vmem] * 4,
        scratch_shapes=[
            pltpu.VMEM((2, ROWS, E), jnp.bfloat16),
            pltpu.VMEM((4, 2, ROWS, E), jnp.bfloat16),
            pltpu.SemaphoreType.DMA((2,)),
            pltpu.SemaphoreType.DMA((3, 2)),
            pltpu.SemaphoreType.DMA((3, 2)),
            pltpu.SemaphoreType.DMA((2, per_kind)),
            pltpu.SemaphoreType.DMA((2, per_kind)),
        ],
        compiler_params=pltpu.CompilerParams(
            collective_id=0, has_side_effects=True, vmem_limit_bytes=40 * 2**20
        ),
        name="window_sums",
    )(img_emb, txt_emb, logit_scale, logit_bias)
    out = jax.ShapeDtypeStruct((ROWS, E), jnp.float32)
    return pl.pallas_call(
        finish_kernel,
        out_shape=(out, out),
        in_specs=[vmem] * 4,
        out_specs=[pl.BlockSpec(memory_space=pl.ANY)] * 2,
        scratch_shapes=[
            pltpu.VMEM((ROWS, E), jnp.float32),
            pltpu.SemaphoreType.DMA((1 + ROWS // FINISH_ROWS,)),
        ],
        compiler_params=pltpu.CompilerParams(vmem_limit_bytes=40 * 2**20),
        name="window_finish",
    )(*(pltpu.with_memory_space_constraint(value, pltpu.VMEM) for value in sums))


def solution(mesh):
    return jax.shard_map(
        functools.partial(per_device, mesh.shape["dx"]),
        mesh=mesh,
        in_specs=(P(("dx", "dy"), None), P(("dx", "dy"), None), P(), P()),
        out_specs=(P(("dx", "dy"), None), P(("dx", "dy"), None)),
        check_vma=False,
    )
```

```python
import functools

import jax
import jax.numpy as jnp
from jax import lax
from jax.experimental import pallas as pl
from jax.experimental.pallas import tpu as pltpu
from jax.sharding import PartitionSpec as P

ROWS = 512
E = 1152
STEP = 256
FINISH_ROWS = 128
LAST_ROWS = 128
IMG, TXT = 0, 1
CORE, Y, X = 0, 1, 2
VMEM_LIMIT = 32 * 2**20
LIGHT = pl.CostEstimate(flops=1000, bytes_accessed=1000, transcendentals=0)


def flipped(index, bit):
    return jnp.where(lax.rem(index // bit, 2) == 1, index - bit, index + bit)


def projected(grads, raw, inverse):
    units = raw.astype(jnp.float32) * inverse
    return inverse * (grads - units * jnp.sum(units * grads, axis=-1, keepdims=True))


def unit_rows(values):
    floats = values.astype(jnp.float32)
    inverse = lax.rsqrt(jnp.sum(floats * floats, axis=-1, keepdims=True) + 1e-06)
    return floats * inverse, inverse


def tile(unit, scale, bias, others, row, diagonal=None):
    logits = scale * lax.dot_general(
        unit[pl.ds(row, STEP), :], others, (((1,), (1,)), ((), ())), preferred_element_type=jnp.float32
    ) + bias
    if diagonal is None:
        coeffs = jax.nn.sigmoid(logits)
    else:
        first = row + lax.broadcasted_iota(jnp.int32, logits.shape, 0)
        second = diagonal + lax.broadcasted_iota(jnp.int32, logits.shape, 1)
        signs = jnp.where(first == second, jnp.float32(1.0), jnp.float32(-1.0))
        coeffs = -signs * jax.nn.sigmoid(-signs * logits)
    return jnp.dot((scale * coeffs).astype(jnp.bfloat16), others, preferred_element_type=jnp.float32)


def add_tiles(sums, unit, scale, bias, far):
    count = STEP if far.shape[0] % STEP == 0 else 128

    @pl.loop(0, far.shape[0] // count)
    def _(step):
        others = unit_rows(far[pl.ds(step * count, count), :])[0].astype(jnp.bfloat16)
        for row in range(0, ROWS, STEP):
            sums[row : row + STEP, :] += tile(unit, scale, bias, others, row)


def near_kernel(img, txt, scale_ref, bias_ref, sum_img, sum_txt, raw, unit, inv, far, load_sem, send_sem, recv_sem):
    dx, dy = lax.axis_index("dx"), lax.axis_index("dy")
    partners = ((flipped(dx, 1), dy), (dx, flipped(dy, 1)), (flipped(dx, 2), dy))
    scale, bias = scale_ref[0], bias_ref[0]
    blocks = (img, txt)
    sums = (sum_img, sum_txt)

    loads = [pltpu.make_async_copy(blocks[kind], raw.at[kind], load_sem.at[kind]) for kind in (IMG, TXT)]
    for load in loads:
        load.start()

    barrier = pltpu.get_barrier_semaphore()
    for partner in partners:
        pl.semaphore_signal(barrier, inc=1, device_id=partner, device_id_type=pl.DeviceIdType.MESH)
    pl.semaphore_wait(barrier, 3)

    copies = {}
    for kind in (TXT, IMG):
        for way in (Y, X, CORE):
            copies[way, kind] = pltpu.make_async_remote_copy(
                src_ref=blocks[kind],
                dst_ref=far.at[way, kind],
                send_sem=send_sem.at[way, kind],
                recv_sem=recv_sem.at[way, kind],
                device_id=partners[way],
                device_id_type=pl.DeviceIdType.MESH,
            )
            copies[way, kind].start()

    for load in loads:
        load.wait()

    @pl.loop(0, ROWS // 128)
    def _(step):
        rows = pl.ds(step * 128, 128)
        for kind in (IMG, TXT):
            units, inverse = unit_rows(raw[kind, rows, :])
            unit[kind, rows, :] = units.astype(jnp.bfloat16)
            inv[kind, rows, :] = inverse

    for kind in (TXT, IMG):
        mine = 1 - kind
        for row in range(0, ROWS, STEP):
            rows = slice(row, row + STEP)
            sums[mine][rows, :] = tile(unit.at[mine], scale, bias, unit[kind, 0:STEP, :], row, 0)
            sums[mine][rows, :] += tile(unit.at[mine], scale, bias, unit[kind, STEP:ROWS, :], row, STEP)

    for way, kind in ((CORE, TXT), (CORE, IMG), (Y, TXT), (X, TXT), (Y, IMG), (X, IMG)):
        copies[way, kind].wait_recv()
        add_tiles(sums[1 - kind], unit.at[1 - kind], scale, bias, far.at[way, kind])

    for copy in copies.values():
        copy.wait_send()


def far_kernel(scale_ref, bias_ref, unit, far, sums_in, sums):
    add_tiles(sums, unit.at[TXT], scale_ref[0], bias_ref[0], far)


def closing_kernel(mine, scale_ref, bias_ref, unit, raw, inv, far, sums, out, grads, sem):
    scale, bias = scale_ref[0], bias_ref[0]
    if far.shape[0] > STEP:
        add_tiles(sums, unit.at[mine], scale, bias, far.at[0 : far.shape[0] - STEP])
        far = far.at[far.shape[0] - STEP : far.shape[0]]
    others = unit_rows(far[...])[0].astype(jnp.bfloat16)
    copies = []
    for row in range(0, ROWS, STEP):
        grads[row : row + STEP, :] = sums[row : row + STEP, :] + tile(unit.at[mine], scale, bias, others, row)
        for first in range(row, row + STEP, FINISH_ROWS):
            rows = pl.ds(first, FINISH_ROWS)
            grads[rows, :] = projected(grads[rows, :], raw[mine, rows, :], inv[mine, rows, :])
            copies.append(pltpu.make_async_copy(grads.at[rows], out.at[rows], sem.at[first // FINISH_ROWS]))
            copies[-1].start()
    for copy in copies:
        copy.wait()


def per_device(n_dx, img_emb, txt_emb, logit_scale, logit_bias):
    vmem = pl.BlockSpec(memory_space=pltpu.VMEM)
    smem = pl.BlockSpec(memory_space=pltpu.SMEM)
    params = pltpu.CompilerParams(vmem_limit_bytes=VMEM_LIMIT)
    scalars = (logit_scale, logit_bias)
    sum_shape = pltpu.VMEM((ROWS, E), jnp.float32)

    def across(value):
        half = n_dx // 2
        return lax.ppermute(value, "dx", [(i, i ^ half) for i in range(n_dx)])

    far_txt = across(txt_emb)
    far_img = across(img_emb[: ROWS - LAST_ROWS])
    far_last = across(img_emb[ROWS - LAST_ROWS :])

    hbm = [pltpu.with_memory_space_constraint(value, pltpu.HBM) for value in (img_emb, txt_emb)]
    sum_img, sum_txt, raw, unit, inv = pl.pallas_call(
        near_kernel,
        out_shape=(
            sum_shape,
            sum_shape,
            pltpu.VMEM((2, ROWS, E), jnp.bfloat16),
            pltpu.VMEM((2, ROWS, E), jnp.bfloat16),
            pltpu.VMEM((2, ROWS, 1), jnp.float32),
        ),
        in_specs=[pl.BlockSpec(memory_space=pltpu.HBM)] * 2 + [smem] * 2,
        out_specs=[vmem] * 5,
        scratch_shapes=[
            pltpu.VMEM((3, 2, ROWS, E), jnp.bfloat16),
            pltpu.SemaphoreType.DMA((2,)),
            pltpu.SemaphoreType.DMA((3, 2)),
            pltpu.SemaphoreType.DMA((3, 2)),
        ],
        compiler_params=pltpu.CompilerParams(collective_id=0, has_side_effects=True, vmem_limit_bytes=VMEM_LIMIT),
        cost_estimate=LIGHT,
        name="near_tiles",
    )(*hbm, *scalars)

    def closing(mine, far, sums, name):
        inputs = [pltpu.with_memory_space_constraint(value, pltpu.VMEM) for value in (unit, raw, inv, far, sums)]
        return pl.pallas_call(
            functools.partial(closing_kernel, mine),
            out_shape=jax.ShapeDtypeStruct((ROWS, E), jnp.float32),
            in_specs=[smem] * 2 + [vmem] * 5,
            out_specs=pl.BlockSpec(memory_space=pl.ANY),
            scratch_shapes=[
                pltpu.VMEM((ROWS, E), jnp.float32),
                pltpu.SemaphoreType.DMA((ROWS // FINISH_ROWS,)),
            ],
            compiler_params=params,
            cost_estimate=LIGHT,
            name=name,
        )(*scalars, *inputs)

    grad_img = closing(IMG, far_txt, sum_img, "close_img")
    grad_img, sum_txt = lax.optimization_barrier((grad_img, sum_txt))
    inputs = [pltpu.with_memory_space_constraint(value, pltpu.VMEM) for value in (unit, far_img, sum_txt)]
    sum_txt = pl.pallas_call(
        far_kernel,
        out_shape=sum_shape,
        in_specs=[smem] * 2 + [vmem] * 3,
        out_specs=vmem,
        input_output_aliases={4: 0},
        compiler_params=params,
        cost_estimate=LIGHT,
        name="far_img_tiles",
    )(*scalars, *inputs)
    grad_txt = closing(TXT, far_last, sum_txt, "close_txt")
    return grad_img, grad_txt


def solution(mesh):
    return jax.shard_map(
        functools.partial(per_device, mesh.shape["dx"]),
        mesh=mesh,
        in_specs=(P(("dx", "dy"), None), P(("dx", "dy"), None), P(), P()),
        out_specs=(P(("dx", "dy"), None), P(("dx", "dy"), None)),
        check_vma=False,
    )
```

```python
import functools

import jax
import jax.numpy as jnp
from jax import lax
from jax.experimental import pallas as pl
from jax.experimental.pallas import tpu as pltpu
from jax.sharding import PartitionSpec as P

ROWS = 512
E = 1152
STEP = 256
FINISH_ROWS = 64
LAST_ROWS = 96
CLOSE_CUTS = (0, 256, 448, 512)
IMG, TXT = 0, 1
CORE, Y, X = 0, 1, 2
VMEM_LIMIT = 32 * 2**20
LIGHT = pl.CostEstimate(flops=1000, bytes_accessed=1000, transcendentals=0)


def flipped(index, bit):
    return jnp.where(lax.rem(index // bit, 2) == 1, index - bit, index + bit)


def projected(grads, raw, inverse):
    units = raw.astype(jnp.float32) * inverse
    return inverse * (grads - units * jnp.sum(units * grads, axis=-1, keepdims=True))


def unit_rows(values):
    floats = values.astype(jnp.float32)
    inverse = lax.rsqrt(jnp.sum(floats * floats, axis=-1, keepdims=True) + 1e-06)
    return floats * inverse, inverse


def tile(unit, scale, bias, others, row, diagonal=None, rows=STEP):
    logits = scale * lax.dot_general(
        unit[pl.ds(row, rows), :], others, (((1,), (1,)), ((), ())), preferred_element_type=jnp.float32
    ) + bias
    if diagonal is None:
        coeffs = jax.nn.sigmoid(logits)
    else:
        first = row + lax.broadcasted_iota(jnp.int32, logits.shape, 0)
        second = diagonal + lax.broadcasted_iota(jnp.int32, logits.shape, 1)
        signs = jnp.where(first == second, jnp.float32(1.0), jnp.float32(-1.0))
        coeffs = -signs * jax.nn.sigmoid(-signs * logits)
    return jnp.dot((scale * coeffs).astype(jnp.bfloat16), others, preferred_element_type=jnp.float32)


def add_tiles(sums, unit, scale, bias, far):
    def add(start, count):
        others = unit_rows(far[pl.ds(start, count), :])[0].astype(jnp.bfloat16)
        for row in range(0, ROWS, STEP):
            sums[row : row + STEP, :] += tile(unit, scale, bias, others, row)

    whole, rest = divmod(far.shape[0], STEP)
    pl.loop(0, whole)(lambda step: add(step * STEP, STEP))
    if rest:
        add(whole * STEP, rest)


def near_kernel(img, txt, scale_ref, bias_ref, sum_img, sum_txt, raw, unit, inv, far, load_sem, send_sem, recv_sem):
    dx, dy = lax.axis_index("dx"), lax.axis_index("dy")
    partners = ((flipped(dx, 1), dy), (dx, flipped(dy, 1)), (flipped(dx, 2), dy))
    scale, bias = scale_ref[0], bias_ref[0]
    blocks = (img, txt)
    sums = (sum_img, sum_txt)

    loads = [pltpu.make_async_copy(blocks[kind], raw.at[kind], load_sem.at[kind]) for kind in (IMG, TXT)]
    for load in loads:
        load.start()

    barrier = pltpu.get_barrier_semaphore()
    for partner in partners:
        pl.semaphore_signal(barrier, inc=1, device_id=partner, device_id_type=pl.DeviceIdType.MESH)
    pl.semaphore_wait(barrier, 3)

    copies = {}
    for kind in (TXT, IMG):
        for way in (Y, X, CORE):
            copies[way, kind] = pltpu.make_async_remote_copy(
                src_ref=blocks[kind],
                dst_ref=far.at[way, kind],
                send_sem=send_sem.at[way, kind],
                recv_sem=recv_sem.at[way, kind],
                device_id=partners[way],
                device_id_type=pl.DeviceIdType.MESH,
            )
            copies[way, kind].start()

    for load in loads:
        load.wait()

    @pl.loop(0, ROWS // 128)
    def _(step):
        rows = pl.ds(step * 128, 128)
        for kind in (IMG, TXT):
            units, inverse = unit_rows(raw[kind, rows, :])
            unit[kind, rows, :] = units.astype(jnp.bfloat16)
            inv[kind, rows, :] = inverse

    for kind in (TXT, IMG):
        mine = 1 - kind
        for row in range(0, ROWS, STEP):
            rows = slice(row, row + STEP)
            sums[mine][rows, :] = tile(unit.at[mine], scale, bias, unit[kind, 0:STEP, :], row, 0)
            sums[mine][rows, :] += tile(unit.at[mine], scale, bias, unit[kind, STEP:ROWS, :], row, STEP)

    for way, kind in ((CORE, TXT), (CORE, IMG), (Y, TXT), (X, TXT), (Y, IMG), (X, IMG)):
        copies[way, kind].wait_recv()
        add_tiles(sums[1 - kind], unit.at[1 - kind], scale, bias, far.at[way, kind])

    for copy in copies.values():
        copy.wait_send()


def far_kernel(scale_ref, bias_ref, unit, far, sums_in, sums):
    add_tiles(sums, unit.at[TXT], scale_ref[0], bias_ref[0], far)


def closing_kernel(mine, scale_ref, bias_ref, unit, raw, inv, sums, far, out, grads, sem):
    scale, bias = scale_ref[0], bias_ref[0]
    count = far.shape[0]
    if count > STEP:
        others = unit_rows(far[0 : count - STEP, :])[0].astype(jnp.bfloat16)
        for row in range(0, ROWS, STEP):
            grads[row : row + STEP, :] = sums[row : row + STEP, :] + tile(unit.at[mine], scale, bias, others, row)
        sums = grads
        far = far.at[count - STEP : count]
    others = unit_rows(far[...])[0].astype(jnp.bfloat16)
    copies = []
    for first, end in zip(CLOSE_CUTS, CLOSE_CUTS[1:]):
        grads[first:end, :] = sums[first:end, :] + tile(unit.at[mine], scale, bias, others, first, rows=end - first)
        for row in range(first, end, FINISH_ROWS):
            rows = pl.ds(row, FINISH_ROWS)
            grads[rows, :] = projected(grads[rows, :], raw[mine, rows, :], inv[mine, rows, :])
        part = pl.ds(first, end - first)
        copies.append(pltpu.make_async_copy(grads.at[part], out.at[part], sem.at[len(copies)]))
        copies[-1].start()
    for copy in copies:
        copy.wait()


def per_device(n_dx, img_emb, txt_emb, logit_scale, logit_bias):
    vmem = pl.BlockSpec(memory_space=pltpu.VMEM)
    smem = pl.BlockSpec(memory_space=pltpu.SMEM)
    params = pltpu.CompilerParams(vmem_limit_bytes=VMEM_LIMIT)
    scalars = (logit_scale, logit_bias)
    sum_shape = pltpu.VMEM((ROWS, E), jnp.float32)

    def across(value):
        half = n_dx // 2
        return lax.ppermute(value, "dx", [(i, i ^ half) for i in range(n_dx)])

    far_txt = across(txt_emb)
    far_img = across(img_emb[: ROWS - LAST_ROWS])
    far_last = across(img_emb[ROWS - LAST_ROWS :])

    hbm = [pltpu.with_memory_space_constraint(value, pltpu.HBM) for value in (img_emb, txt_emb)]
    sum_img, sum_txt, raw, unit, inv = pl.pallas_call(
        near_kernel,
        out_shape=(
            sum_shape,
            sum_shape,
            pltpu.VMEM((2, ROWS, E), jnp.bfloat16),
            pltpu.VMEM((2, ROWS, E), jnp.bfloat16),
            pltpu.VMEM((2, ROWS, 1), jnp.float32),
        ),
        in_specs=[pl.BlockSpec(memory_space=pltpu.HBM)] * 2 + [smem] * 2,
        out_specs=[vmem] * 5,
        scratch_shapes=[
            pltpu.VMEM((3, 2, ROWS, E), jnp.bfloat16),
            pltpu.SemaphoreType.DMA((2,)),
            pltpu.SemaphoreType.DMA((3, 2)),
            pltpu.SemaphoreType.DMA((3, 2)),
        ],
        compiler_params=pltpu.CompilerParams(collective_id=0, has_side_effects=True, vmem_limit_bytes=VMEM_LIMIT),
        cost_estimate=LIGHT,
        name="near_tiles",
    )(*hbm, *scalars)

    def closing(mine, far, sums, name):
        inputs = [pltpu.with_memory_space_constraint(value, pltpu.VMEM) for value in (unit, raw, inv, sums, far)]
        return pl.pallas_call(
            functools.partial(closing_kernel, mine),
            out_shape=jax.ShapeDtypeStruct((ROWS, E), jnp.float32),
            in_specs=[smem] * 2 + [vmem] * 5,
            out_specs=pl.BlockSpec(memory_space=pl.ANY),
            scratch_shapes=[
                pltpu.VMEM((ROWS, E), jnp.float32),
                pltpu.SemaphoreType.DMA((len(CLOSE_CUTS) - 1,)),
            ],
            compiler_params=params,
            cost_estimate=LIGHT,
            name=name,
        )(*scalars, *inputs)

    grad_img = closing(IMG, far_txt, sum_img, "close_img")
    grad_img, sum_txt = lax.optimization_barrier((grad_img, sum_txt))
    inputs = [pltpu.with_memory_space_constraint(value, pltpu.VMEM) for value in (unit, far_img, sum_txt)]
    sum_txt = pl.pallas_call(
        far_kernel,
        out_shape=sum_shape,
        in_specs=[smem] * 2 + [vmem] * 3,
        out_specs=vmem,
        input_output_aliases={4: 0},
        compiler_params=params,
        cost_estimate=LIGHT,
        name="far_img_tiles",
    )(*scalars, *inputs)
    grad_txt = closing(TXT, far_last, sum_txt, "close_txt")
    return grad_img, grad_txt


def solution(mesh):
    return jax.shard_map(
        functools.partial(per_device, mesh.shape["dx"]),
        mesh=mesh,
        in_specs=(P(("dx", "dy"), None), P(("dx", "dy"), None), P(), P()),
        out_specs=(P(("dx", "dy"), None), P(("dx", "dy"), None)),
        check_vma=False,
    )
```

```python
import functools

import jax
import jax.numpy as jnp
from jax import lax
from jax.experimental import pallas as pl
from jax.experimental.pallas import tpu as pltpu
from jax.sharding import PartitionSpec as P

ROWS = 512
E = 1152
STEP = 256
FINISH_ROWS = 64
LAST_ROWS = 128
CLOSE_CUTS = (0, 256, 448, 512)
IMG, TXT = 0, 1
CORE, Y, X = 0, 1, 2
VMEM_LIMIT = 32 * 2**20
LIGHT = pl.CostEstimate(flops=1000, bytes_accessed=1000, transcendentals=0)


def flipped(index, bit):
    return jnp.where(lax.rem(index // bit, 2) == 1, index - bit, index + bit)


def projected(grads, raw, inverse):
    units = raw.astype(jnp.float32) * inverse
    return inverse * (grads - units * jnp.sum(units * grads, axis=-1, keepdims=True))


def unit_rows(values):
    floats = values.astype(jnp.float32)
    inverse = lax.rsqrt(jnp.sum(floats * floats, axis=-1, keepdims=True) + 1e-06)
    return floats * inverse, inverse


def tile(unit, scale, bias, others, row, diagonal=None, rows=STEP):
    logits = scale * lax.dot_general(
        unit[pl.ds(row, rows), :], others, (((1,), (1,)), ((), ())), preferred_element_type=jnp.float32
    ) + bias
    if diagonal is None:
        coeffs = jax.nn.sigmoid(logits)
    else:
        first = row + lax.broadcasted_iota(jnp.int32, logits.shape, 0)
        second = diagonal + lax.broadcasted_iota(jnp.int32, logits.shape, 1)
        signs = jnp.where(first == second, jnp.float32(1.0), jnp.float32(-1.0))
        coeffs = -signs * jax.nn.sigmoid(-signs * logits)
    return jnp.dot((scale * coeffs).astype(jnp.bfloat16), others, preferred_element_type=jnp.float32)


def add_tiles(sums, unit, scale, bias, far):
    def add(start, count):
        others = unit_rows(far[pl.ds(start, count), :])[0].astype(jnp.bfloat16)
        for row in range(0, ROWS, STEP):
            sums[row : row + STEP, :] += tile(unit, scale, bias, others, row)

    whole, rest = divmod(far.shape[0], STEP)
    pl.loop(0, whole)(lambda step: add(step * STEP, STEP))
    if rest:
        add(whole * STEP, rest)


def near_kernel(img, txt, scale_ref, bias_ref, sum_img, sum_txt, raw, unit, inv, far, load_sem, send_sem, recv_sem):
    dx, dy = lax.axis_index("dx"), lax.axis_index("dy")
    partners = ((flipped(dx, 1), dy), (dx, flipped(dy, 1)), (flipped(dx, 2), dy))
    scale, bias = scale_ref[0], bias_ref[0]
    blocks = (img, txt)
    sums = (sum_img, sum_txt)

    loads = [pltpu.make_async_copy(blocks[kind], raw.at[kind], load_sem.at[kind]) for kind in (IMG, TXT)]
    for load in loads:
        load.start()

    barrier = pltpu.get_barrier_semaphore()
    for partner in partners:
        pl.semaphore_signal(barrier, inc=1, device_id=partner, device_id_type=pl.DeviceIdType.MESH)
    pl.semaphore_wait(barrier, 3)

    copies = {}
    for kind in (TXT, IMG):
        for way in (Y, X, CORE):
            copies[way, kind] = pltpu.make_async_remote_copy(
                src_ref=blocks[kind],
                dst_ref=far.at[way, kind],
                send_sem=send_sem.at[way, kind],
                recv_sem=recv_sem.at[way, kind],
                device_id=partners[way],
                device_id_type=pl.DeviceIdType.MESH,
            )
            copies[way, kind].start()

    for load in loads:
        load.wait()

    @pl.loop(0, ROWS // 128)
    def _(step):
        rows = pl.ds(step * 128, 128)
        for kind in (IMG, TXT):
            units, inverse = unit_rows(raw[kind, rows, :])
            unit[kind, rows, :] = units.astype(jnp.bfloat16)
            inv[kind, rows, :] = inverse

    for kind in (TXT, IMG):
        mine = 1 - kind
        for row in range(0, ROWS, STEP):
            rows = slice(row, row + STEP)
            sums[mine][rows, :] = tile(unit.at[mine], scale, bias, unit[kind, 0:STEP, :], row, 0)
            sums[mine][rows, :] += tile(unit.at[mine], scale, bias, unit[kind, STEP:ROWS, :], row, STEP)

    for way, kind in ((CORE, TXT), (CORE, IMG), (Y, TXT), (X, TXT), (Y, IMG), (X, IMG)):
        copies[way, kind].wait_recv()
        add_tiles(sums[1 - kind], unit.at[1 - kind], scale, bias, far.at[way, kind])

    for copy in copies.values():
        copy.wait_send()


def far_kernel(scale_ref, bias_ref, unit, far, sums_in, sums):
    add_tiles(sums, unit.at[TXT], scale_ref[0], bias_ref[0], far)


def closing_kernel(mine, scale_ref, bias_ref, unit, raw, inv, sums, far, out, grads, sem):
    scale, bias = scale_ref[0], bias_ref[0]
    count = far.shape[0]
    if count > STEP:
        others = unit_rows(far[0 : count - STEP, :])[0].astype(jnp.bfloat16)
        for row in range(0, ROWS, STEP):
            grads[row : row + STEP, :] = sums[row : row + STEP, :] + tile(unit.at[mine], scale, bias, others, row)
        sums = grads
        far = far.at[count - STEP : count]
    others = far[...]
    inverse = unit_rows(others)[1]
    inverse = jnp.broadcast_to(inverse, (inverse.shape[0], 128)).T[0:1, :]
    copies = []
    for first, end in zip(CLOSE_CUTS, CLOSE_CUTS[1:]):
        dots = lax.dot_general(
            unit[mine, first:end, :], others, (((1,), (1,)), ((), ())), preferred_element_type=jnp.float32
        )
        coeffs = scale * jax.nn.sigmoid(dots * (scale * inverse) + bias) * inverse
        more = jnp.dot(coeffs.astype(jnp.bfloat16), others, preferred_element_type=jnp.float32)
        grads[first:end, :] = sums[first:end, :] + more
        for row in range(first, end, FINISH_ROWS):
            rows = pl.ds(row, FINISH_ROWS)
            grads[rows, :] = projected(grads[rows, :], raw[mine, rows, :], inv[mine, rows, :])
        part = pl.ds(first, end - first)
        copies.append(pltpu.make_async_copy(grads.at[part], out.at[part], sem.at[len(copies)]))
        copies[-1].start()
    for copy in copies:
        copy.wait()


def per_device(n_dx, img_emb, txt_emb, logit_scale, logit_bias):
    vmem = pl.BlockSpec(memory_space=pltpu.VMEM)
    smem = pl.BlockSpec(memory_space=pltpu.SMEM)
    params = pltpu.CompilerParams(vmem_limit_bytes=VMEM_LIMIT)
    scalars = (logit_scale, logit_bias)
    sum_shape = pltpu.VMEM((ROWS, E), jnp.float32)

    def across(value):
        half = n_dx // 2
        return lax.ppermute(value, "dx", [(i, i ^ half) for i in range(n_dx)])

    far_txt = across(txt_emb)
    far_img = across(img_emb[: ROWS - LAST_ROWS])
    far_last = across(img_emb[ROWS - LAST_ROWS :])

    hbm = [pltpu.with_memory_space_constraint(value, pltpu.HBM) for value in (img_emb, txt_emb)]
    sum_img, sum_txt, raw, unit, inv = pl.pallas_call(
        near_kernel,
        out_shape=(
            sum_shape,
            sum_shape,
            pltpu.VMEM((2, ROWS, E), jnp.bfloat16),
            pltpu.VMEM((2, ROWS, E), jnp.bfloat16),
            pltpu.VMEM((2, ROWS, 1), jnp.float32),
        ),
        in_specs=[pl.BlockSpec(memory_space=pltpu.HBM)] * 2 + [smem] * 2,
        out_specs=[vmem] * 5,
        scratch_shapes=[
            pltpu.VMEM((3, 2, ROWS, E), jnp.bfloat16),
            pltpu.SemaphoreType.DMA((2,)),
            pltpu.SemaphoreType.DMA((3, 2)),
            pltpu.SemaphoreType.DMA((3, 2)),
        ],
        compiler_params=pltpu.CompilerParams(collective_id=0, has_side_effects=True, vmem_limit_bytes=VMEM_LIMIT),
        cost_estimate=LIGHT,
        name="near_tiles",
    )(*hbm, *scalars)

    def closing(mine, far, sums, name):
        inputs = [pltpu.with_memory_space_constraint(value, pltpu.VMEM) for value in (unit, raw, inv, sums, far)]
        return pl.pallas_call(
            functools.partial(closing_kernel, mine),
            out_shape=jax.ShapeDtypeStruct((ROWS, E), jnp.float32),
            in_specs=[smem] * 2 + [vmem] * 5,
            out_specs=pl.BlockSpec(memory_space=pl.ANY),
            scratch_shapes=[
                pltpu.VMEM((ROWS, E), jnp.float32),
                pltpu.SemaphoreType.DMA((len(CLOSE_CUTS) - 1,)),
            ],
            compiler_params=params,
            cost_estimate=LIGHT,
            name=name,
        )(*scalars, *inputs)

    grad_img = closing(IMG, far_txt, sum_img, "close_img")
    grad_img, sum_txt = lax.optimization_barrier((grad_img, sum_txt))
    inputs = [pltpu.with_memory_space_constraint(value, pltpu.VMEM) for value in (unit, far_img, sum_txt)]
    sum_txt = pl.pallas_call(
        far_kernel,
        out_shape=sum_shape,
        in_specs=[smem] * 2 + [vmem] * 3,
        out_specs=vmem,
        input_output_aliases={4: 0},
        compiler_params=params,
        cost_estimate=LIGHT,
        name="far_img_tiles",
    )(*scalars, *inputs)
    grad_txt = closing(TXT, far_last, sum_txt, "close_txt")
    return grad_img, grad_txt


def solution(mesh):
    return jax.shard_map(
        functools.partial(per_device, mesh.shape["dx"]),
        mesh=mesh,
        in_specs=(P(("dx", "dy"), None), P(("dx", "dy"), None), P(), P()),
        out_specs=(P(("dx", "dy"), None), P(("dx", "dy"), None)),
        check_vma=False,
    )
```

```python
import functools

import jax
import jax.numpy as jnp
from jax import lax
from jax.experimental import pallas as pl
from jax.experimental.pallas import tpu as pltpu
from jax.sharding import PartitionSpec as P

ROWS = 512
E = 1152
STEP = 256
FINISH_ROWS = 64
LAST_ROWS = 96
CLOSE_CUTS = (0, 256, 448, 512)
IMG, TXT = 0, 1
CORE, Y, X = 0, 1, 2
VMEM_LIMIT = 32 * 2**20
LIGHT = pl.CostEstimate(flops=1000, bytes_accessed=1000, transcendentals=0)


def flipped(index, bit):
    return jnp.where(lax.rem(index // bit, 2) == 1, index - bit, index + bit)


def projected(grads, raw, inverse):
    units = raw.astype(jnp.float32) * inverse
    return inverse * (grads - units * jnp.sum(units * grads, axis=-1, keepdims=True))


def unit_rows(values):
    floats = values.astype(jnp.float32)
    inverse = lax.rsqrt(jnp.sum(floats * floats, axis=-1, keepdims=True) + 1e-06)
    return floats * inverse, inverse


def tile(unit, scale, bias, others, row, diagonal=None, rows=STEP):
    logits = scale * lax.dot_general(
        unit[pl.ds(row, rows), :], others, (((1,), (1,)), ((), ())), preferred_element_type=jnp.float32
    ) + bias
    if diagonal is None:
        coeffs = jax.nn.sigmoid(logits)
    else:
        first = row + lax.broadcasted_iota(jnp.int32, logits.shape, 0)
        second = diagonal + lax.broadcasted_iota(jnp.int32, logits.shape, 1)
        signs = jnp.where(first == second, jnp.float32(1.0), jnp.float32(-1.0))
        coeffs = -signs * jax.nn.sigmoid(-signs * logits)
    return jnp.dot((scale * coeffs).astype(jnp.bfloat16), others, preferred_element_type=jnp.float32)


def add_tiles(sums, unit, scale, bias, far):
    def add(start, count):
        others = unit_rows(far[pl.ds(start, count), :])[0].astype(jnp.bfloat16)
        for row in range(0, ROWS, STEP):
            sums[row : row + STEP, :] += tile(unit, scale, bias, others, row)

    whole, rest = divmod(far.shape[0], STEP)
    pl.loop(0, whole)(lambda step: add(step * STEP, STEP))
    if rest:
        add(whole * STEP, rest)


def near_kernel(img, txt, scale_ref, bias_ref, sum_img, sum_txt, raw, unit, inv, far, load_sem, send_sem, recv_sem):
    dx, dy = lax.axis_index("dx"), lax.axis_index("dy")
    partners = ((flipped(dx, 1), dy), (dx, flipped(dy, 1)), (flipped(dx, 2), dy))
    scale, bias = scale_ref[0], bias_ref[0]
    blocks = (img, txt)
    sums = (sum_img, sum_txt)

    loads = [pltpu.make_async_copy(blocks[kind], raw.at[kind], load_sem.at[kind]) for kind in (IMG, TXT)]
    for load in loads:
        load.start()

    barrier = pltpu.get_barrier_semaphore()
    for partner in partners:
        pl.semaphore_signal(barrier, inc=1, device_id=partner, device_id_type=pl.DeviceIdType.MESH)
    pl.semaphore_wait(barrier, 3)

    copies = {}
    for kind in (TXT, IMG):
        for way in (Y, X, CORE):
            copies[way, kind] = pltpu.make_async_remote_copy(
                src_ref=blocks[kind],
                dst_ref=far.at[way, kind],
                send_sem=send_sem.at[way, kind],
                recv_sem=recv_sem.at[way, kind],
                device_id=partners[way],
                device_id_type=pl.DeviceIdType.MESH,
            )
            copies[way, kind].start()

    for load in loads:
        load.wait()

    @pl.loop(0, ROWS // 128)
    def _(step):
        rows = pl.ds(step * 128, 128)
        for kind in (IMG, TXT):
            units, inverse = unit_rows(raw[kind, rows, :])
            unit[kind, rows, :] = units.astype(jnp.bfloat16)
            inv[kind, rows, :] = inverse

    for kind in (TXT, IMG):
        mine = 1 - kind
        for row in range(0, ROWS, STEP):
            rows = slice(row, row + STEP)
            sums[mine][rows, :] = tile(unit.at[mine], scale, bias, unit[kind, 0:STEP, :], row, 0)
            sums[mine][rows, :] += tile(unit.at[mine], scale, bias, unit[kind, STEP:ROWS, :], row, STEP)

    for way, kind in ((CORE, TXT), (CORE, IMG), (Y, TXT), (X, TXT), (Y, IMG), (X, IMG)):
        copies[way, kind].wait_recv()
        add_tiles(sums[1 - kind], unit.at[1 - kind], scale, bias, far.at[way, kind])

    for copy in copies.values():
        copy.wait_send()


def far_kernel(scale_ref, bias_ref, unit, far, sums_in, sums):
    add_tiles(sums, unit.at[TXT], scale_ref[0], bias_ref[0], far)


def closing_kernel(mine, scale_ref, bias_ref, unit, raw, inv, sums, far, out, grads, sem):
    scale, bias = scale_ref[0], bias_ref[0]
    count = far.shape[0]
    if count > STEP:
        others = unit_rows(far[0 : count - STEP, :])[0].astype(jnp.bfloat16)
        for row in range(0, ROWS, STEP):
            grads[row : row + STEP, :] = sums[row : row + STEP, :] + tile(unit.at[mine], scale, bias, others, row)
        sums = grads
        far = far.at[count - STEP : count]
    others = far[...]
    inverse = unit_rows(others)[1]
    inverse = jnp.broadcast_to(inverse, (inverse.shape[0], 128)).T[0:1, :]
    copies = []
    for first, end in zip(CLOSE_CUTS, CLOSE_CUTS[1:]):
        dots = lax.dot_general(
            unit[mine, first:end, :], others, (((1,), (1,)), ((), ())), preferred_element_type=jnp.float32
        )
        coeffs = scale * jax.nn.sigmoid(dots * (scale * inverse) + bias) * inverse
        more = jnp.dot(coeffs.astype(jnp.bfloat16), others, preferred_element_type=jnp.float32)
        grads[first:end, :] = sums[first:end, :] + more
        for row in range(first, end, FINISH_ROWS):
            rows = pl.ds(row, FINISH_ROWS)
            grads[rows, :] = projected(grads[rows, :], raw[mine, rows, :], inv[mine, rows, :])
        part = pl.ds(first, end - first)
        copies.append(pltpu.make_async_copy(grads.at[part], out.at[part], sem.at[len(copies)]))
        copies[-1].start()
    for copy in copies:
        copy.wait()


def per_device(n_dx, img_emb, txt_emb, logit_scale, logit_bias):
    vmem = pl.BlockSpec(memory_space=pltpu.VMEM)
    smem = pl.BlockSpec(memory_space=pltpu.SMEM)
    params = pltpu.CompilerParams(vmem_limit_bytes=VMEM_LIMIT)
    scalars = (logit_scale, logit_bias)
    sum_shape = pltpu.VMEM((ROWS, E), jnp.float32)

    def across(value):
        half = n_dx // 2
        return lax.ppermute(value, "dx", [(i, i ^ half) for i in range(n_dx)])

    far_txt = across(txt_emb)
    far_img = across(img_emb[: ROWS - LAST_ROWS])
    far_last = across(img_emb[ROWS - LAST_ROWS :])

    hbm = [pltpu.with_memory_space_constraint(value, pltpu.HBM) for value in (img_emb, txt_emb)]
    sum_img, sum_txt, raw, unit, inv = pl.pallas_call(
        near_kernel,
        out_shape=(
            sum_shape,
            sum_shape,
            pltpu.VMEM((2, ROWS, E), jnp.bfloat16),
            pltpu.VMEM((2, ROWS, E), jnp.bfloat16),
            pltpu.VMEM((2, ROWS, 1), jnp.float32),
        ),
        in_specs=[pl.BlockSpec(memory_space=pltpu.HBM)] * 2 + [smem] * 2,
        out_specs=[vmem] * 5,
        scratch_shapes=[
            pltpu.VMEM((3, 2, ROWS, E), jnp.bfloat16),
            pltpu.SemaphoreType.DMA((2,)),
            pltpu.SemaphoreType.DMA((3, 2)),
            pltpu.SemaphoreType.DMA((3, 2)),
        ],
        compiler_params=pltpu.CompilerParams(collective_id=0, has_side_effects=True, vmem_limit_bytes=VMEM_LIMIT),
        cost_estimate=LIGHT,
        name="near_tiles",
    )(*hbm, *scalars)

    def closing(mine, far, sums, name):
        inputs = [pltpu.with_memory_space_constraint(value, pltpu.VMEM) for value in (unit, raw, inv, sums, far)]
        return pl.pallas_call(
            functools.partial(closing_kernel, mine),
            out_shape=jax.ShapeDtypeStruct((ROWS, E), jnp.float32),
            in_specs=[smem] * 2 + [vmem] * 5,
            out_specs=pl.BlockSpec(memory_space=pl.ANY),
            scratch_shapes=[
                pltpu.VMEM((ROWS, E), jnp.float32),
                pltpu.SemaphoreType.DMA((len(CLOSE_CUTS) - 1,)),
            ],
            compiler_params=params,
            cost_estimate=LIGHT,
            name=name,
        )(*scalars, *inputs)

    grad_img = closing(IMG, far_txt, sum_img, "close_img")
    grad_img, sum_txt = lax.optimization_barrier((grad_img, sum_txt))
    inputs = [pltpu.with_memory_space_constraint(value, pltpu.VMEM) for value in (unit, far_img, sum_txt)]
    sum_txt = pl.pallas_call(
        far_kernel,
        out_shape=sum_shape,
        in_specs=[smem] * 2 + [vmem] * 3,
        out_specs=vmem,
        input_output_aliases={4: 0},
        compiler_params=params,
        cost_estimate=LIGHT,
        name="far_img_tiles",
    )(*scalars, *inputs)
    grad_txt = closing(TXT, far_last, sum_txt, "close_txt")
    return grad_img, grad_txt


def solution(mesh):
    return jax.shard_map(
        functools.partial(per_device, mesh.shape["dx"]),
        mesh=mesh,
        in_specs=(P(("dx", "dy"), None), P(("dx", "dy"), None), P(), P()),
        out_specs=(P(("dx", "dy"), None), P(("dx", "dy"), None)),
        check_vma=False,
    )
```
